128 devices in a mesh: blk: 16 (over z_hi, x, core), order: 8 (over z_lo, y).
Axes of the slice: x: 4, y: 4, z: 4 (z_hi: 2, z_lo: 2; z = z_hi * 2 + z_lo), core: 2. Of those that a mesh axis runs over, the one named last changes fastest.
Arguments:
- fourier: bfloat16 [16, 128, 32768], P(None, None, ('blk', 'order')), may hold values from -6 to 6
- cycle_lat: int32 [32768], replicated, may hold values from 0 to 32767, as said below
- order_table: int32 [128], replicated, may hold values from 0 to 127, each once
- leaf_op: bfloat16 [128, 128, 32768], P('order', None, 'blk'), may hold values from -0.125 to 0.125
- level_op: bfloat16 [4, 16, 128, 128, 256], P(None, 'blk', 'order'), may hold values from -0.25 to 0.25
- skeleton: int32 [4, 16, 128, 128], P(None, 'blk', 'order'), may hold values from 0 to 255, as said below
- top_op: bfloat16 [128, 16384, 128], P('order', 'blk'), may hold values from -0.5 to 0.5
Outputs:
- alm: float32 [16, 128, 16384], P(None, 'order', 'blk')
The draws below stay inside these ranges and needn't reach their ends.
Inputs may be any that keep to these rules, and one draw needn't show every extreme that they name: `cycle_lat`: a permutation of the cycles; the 256 stored cycles of each device hold exactly 16 cycles of each leaf block. `skeleton`: each list holds 128 distinct entries.
All inputs are finite; a program needn't handle non-finite values.
Results may differ from the reference program's by a relative error of at most 0.0065.
Values may be sent and summed in bfloat16 or wider, within the bound.
A program may use at most 128 MiB of HBM per device.

```python
import jax
import jax.numpy as jnp
from jax import lax

L = 16384
CYCLES = 32768
KRANK = 128
COLS = 16
ORDERS = 128
LEVELS = 4
RB = 2048
LB = 1024
ROWS_DEV = 256
RPB = 16
N_BLK = 16
DEVICES = 128


def draw_cycle_lat(key, part):
    key = jax.random.fold_in(key, 11)
    first, second = jax.random.split(key)
    block_keys = jax.random.split(first, N_BLK)
    shuffled = jax.vmap(lambda k: jax.random.permutation(k, RB))(block_keys).astype(jnp.int32)
    lat = shuffled + (jnp.arange(N_BLK, dtype=jnp.int32) * RB)[:, None]
    lat = lat.reshape(N_BLK, DEVICES, RPB).transpose(1, 0, 2).reshape(DEVICES, ROWS_DEV)
    row_keys = jax.random.split(second, DEVICES)
    lat = jax.vmap(lambda k, row: jax.random.permutation(k, row))(row_keys, lat)
    return lat.reshape(CYCLES).astype(jnp.int32)


def draw_skeleton(key, part):
    key = jax.random.fold_in(key, 23)
    count = LEVELS * N_BLK * ORDERS
    list_keys = jax.random.split(key, count)
    lists = jax.vmap(lambda k: jax.random.permutation(k, 2 * KRANK)[:KRANK])(list_keys)
    return lists.reshape(LEVELS, N_BLK, ORDERS, KRANK).astype(jnp.int32)


def level_of(rng, dims, cuts, least, largest):
    factor_of, own = 1.0, jax.random.fold_in(rng, 6)
    for position, parts in cuts:
        steps = jnp.exp(jax.random.uniform(jax.random.fold_in(own, position), (parts,), jnp.float32, least / len(cuts), largest / len(cuts)))
        factor_of = factor_of * jnp.repeat(steps, dims[position] // parts).reshape([-1 if axis == position else 1 for axis in range(len(dims))])
    return factor_of


def gaussian(own_key, shape, scale, bound, cuts=(), kind=jnp.bfloat16):
    array = scale * jax.random.normal(own_key, shape, jnp.float32)
    if cuts:
        array = array * level_of(own_key, shape, cuts, -0.22, 0.18)
    return jnp.clip(array, -bound, bound).astype(kind)


def setup_inputs(seed: int = 0) -> dict:
    keys = jax.random.split(jax.random.key(seed), 8)
    return {
        "fourier": gaussian(keys[0], (COLS, ORDERS, CYCLES), 1.0, 6.0, ((2, 128),)),
        "cycle_lat": draw_cycle_lat(jax.random.fold_in(keys[7], 71), 0),
        "order_table": jax.random.permutation(keys[2], ORDERS).astype(jnp.int32),
        "leaf_op": gaussian(keys[3], (ORDERS, KRANK, CYCLES), RB ** -0.5, 0.125, ((0, 8), (2, 16))),
        "level_op": gaussian(keys[4], (LEVELS, N_BLK, ORDERS, KRANK, 2 * KRANK), (4 * KRANK) ** -0.5, 0.25, ((1, 16), (2, 8))),
        "skeleton": draw_skeleton(jax.random.fold_in(keys[7], 71), 0),
        "top_op": gaussian(keys[6], (ORDERS, L, KRANK), KRANK ** -0.5, 0.5, ((0, 8), (1, 16))),
    }


def reference(fourier, cycle_lat, order_table, leaf_op, level_op, skeleton, top_op):
    inverse = jnp.argsort(cycle_lat).astype(jnp.int32)
    ordered = jnp.take(jnp.take(fourier, order_table, axis=1), inverse, axis=2)
    block_ids = jnp.arange(N_BLK, dtype=jnp.int32)

    def one_slot(slot):
        field = lax.dynamic_index_in_dim(ordered, slot, 1, keepdims=False).astype(jnp.float32).reshape(COLS, N_BLK, RB)
        leaf = lax.dynamic_index_in_dim(leaf_op, slot, 0, keepdims=False).astype(jnp.float32).reshape(KRANK, N_BLK, RB)
        coeff = jnp.einsum("kbr,cbr->bck", leaf, field).astype(jnp.bfloat16)
        for level in range(LEVELS):
            partner = jnp.take(coeff, jnp.bitwise_xor(block_ids, 2 ** level), axis=0)
            combined = jnp.concatenate([coeff, partner], axis=2)
            chosen = lax.dynamic_index_in_dim(skeleton[level], slot, 1, keepdims=False)
            picked = jnp.take_along_axis(combined, chosen[:, None, :], axis=2)
            mixing = lax.dynamic_index_in_dim(level_op[level], slot, 1, keepdims=False).astype(jnp.float32)
            product = jnp.einsum("bkq,bcq->bck", mixing, combined.astype(jnp.float32))
            coeff = (picked.astype(jnp.float32) + product).astype(jnp.bfloat16)
        expand = lax.dynamic_index_in_dim(top_op, slot, 0, keepdims=False).astype(jnp.float32).reshape(N_BLK, LB, KRANK)
        return jnp.einsum("blk,bck->cbl", expand, coeff.astype(jnp.float32)).reshape(COLS, L)

    result = lax.map(one_slot, jnp.arange(ORDERS, dtype=jnp.int32))
    return jnp.transpose(result, (1, 0, 2))
```

```python
import functools

import jax
import jax.numpy as jnp
from jax import lax
from jax.experimental import pallas as pl
from jax.experimental.pallas import tpu as pltpu
from jax.sharding import PartitionSpec as P

MESH = pl.DeviceIdType.MESH
BLKS, OWNERS, DEVICES = 16, 8, 128
COLS, ORDERS, ROWS, RPB = 16, 128, 256, 16
SLOTS, HALF, GROUPS = 16, 8, 2
RB, LB, KR, LEVELS = 2048, 1024, 128, 4
RB_SHIFT = 11
WIDE = COLS * HALF
CHUNKS = 8
BF, F32, I32 = jnp.bfloat16, jnp.float32, jnp.int32


def hops(k):
    kb, ko = k // OWNERS, k % OWNERS
    z = (kb >> 3) * 2 + (ko >> 2)
    ring = (0, 1, 2, 1)
    return ring[(kb >> 1) & 3] + ring[z] + ring[ko & 3]


PARTNERS = sorted(range(DEVICES), key=lambda k: (-hops(k), (k * 37) % DEVICES))
PARTNERS.remove(0)
PARTNERS.append(0)


def iota(shape, dim):
    return lax.broadcasted_iota(I32, shape, dim)


def ones_where(mask):
    return jnp.where(mask, 1.0, 0.0).astype(F32)


def dot(a, b):
    return jnp.dot(a, b, preferred_element_type=F32)


def dot_nt(a, b):
    return lax.dot_general(a, b, (((1,), (1,)), ((), ())), preferred_element_type=F32)


def kernel(
    fourier, lat, otab, leaf, level, skel, top, korder, out,
    fv, latv, otabv, leafv, mixv, skelv, topv, kordv, outv,
    wide, sendb, recvb, placing, total, field, products, comb,
    in_sem, send_sem, recv_sem, own_sem, x_send, x_recv, out_sem,
):
    b, o = lax.axis_index("blk"), lax.axis_index("order")
    me = b * OWNERS + o

    loads = [
        pltpu.make_async_copy(lat, latv, in_sem.at[0]),
        pltpu.make_async_copy(otab, otabv, in_sem.at[1]),
        pltpu.make_async_copy(fourier, fv, in_sem.at[2]),
        pltpu.make_async_copy(korder, kordv, in_sem.at[3]),
        pltpu.make_async_copy(skel, skelv, in_sem.at[4]),
        pltpu.make_async_copy(leaf, leafv, in_sem.at[5]),
        pltpu.make_async_copy(level, mixv.at[:, :, :, pl.ds(0, 2 * KR)], in_sem.at[6]),
    ]
    for s in range(SLOTS):
        loads.append(pltpu.make_async_copy(top.at[s], topv.at[:, pl.ds(s * KR, KR)], in_sem.at[7 + s]))
    for copy in loads[:3]:
        copy.start()

    barrier = pltpu.get_barrier_semaphore()

    def greet(i, carry):
        pl.semaphore_signal(
            barrier, inc=1, device_id=(b ^ (i // OWNERS), o ^ (i % OWNERS)), device_id_type=MESH
        )
        return carry

    lax.fori_loop(1, DEVICES, greet, 0)
    for copy in loads[3:]:
        copy.start()

    loads[0].wait()
    own = jnp.concatenate([latv[pl.ds(2 * me, 1), :], latv[pl.ds(2 * me + 1, 1), :]], axis=1)
    own_block = own >> RB_SHIFT
    in_block = ones_where(iota((BLKS, ROWS), 0) == own_block)
    earlier = ones_where(iota((ROWS, ROWS), 0) < iota((ROWS, ROWS), 1)).astype(BF)
    rank = jnp.sum(in_block * dot(in_block.astype(BF), earlier), axis=0, keepdims=True)
    target = own_block * RPB + rank.astype(I32)
    row_pick = ones_where(iota((ROWS, ROWS), 0) == target).astype(BF)

    loads[1].wait()
    order_pick = jnp.transpose(ones_where(iota((ORDERS, ORDERS), 0) == otabv[...])).astype(BF)
    loads[2].wait()
    for c in range(COLS):
        by_slot = dot(order_pick, fv[c])
        wide[:, c * HALF:(c + 1) * HALF, :] = by_slot.reshape(OWNERS * GROUPS, HALF, ROWS)

    def sort_rows(i, carry):
        both = wide[pl.ds(GROUPS * i, GROUPS)].reshape(GROUPS * WIDE, ROWS).astype(BF)
        rows = dot_nt(row_pick, both).astype(BF)
        for g in range(GROUPS):
            sendb[g, i] = rows[:, g * WIDE:(g + 1) * WIDE]
        return carry

    lax.fori_loop(0, OWNERS, sort_rows, 0)

    pl.semaphore_wait(barrier, DEVICES - 1)
    for g in range(GROUPS):
        for t, k in enumerate(PARTNERS):
            kb, ko = b ^ (k // OWNERS), o ^ (k % OWNERS)
            src = sendb.at[g, ko, pl.ds(kb * RPB, RPB), :]
            dst = recvb.at[g, pl.ds(t * RPB, RPB), :]
            if k == 0:
                pltpu.make_async_copy(src, dst, own_sem.at[g]).start()
            else:
                pltpu.make_async_remote_copy(
                    src, dst, send_sem, recv_sem.at[g, t // (DEVICES // CHUNKS)],
                    device_id=(kb, ko), device_id_type=MESH,
                ).start()

    lat_t = jnp.concatenate(
        [jnp.transpose(latv[pl.ds(h, DEVICES, stride=2), :].astype(F32)) for h in range(2)], axis=0
    ).astype(I32)
    here = (lat_t >> RB_SHIFT) == b
    local = lat_t & (RB - 1)
    later = ones_where(iota((ROWS, ROWS), 1) < iota((ROWS, ROWS), 0)).astype(BF)
    ranks = dot(later, ones_where(here).astype(BF)).astype(I32)
    ranks = jnp.where(here, ranks, -1)
    by_rank = jnp.concatenate(
        [jnp.sum(jnp.where(ranks == p, local, 0), axis=0, keepdims=True) for p in range(RPB)], axis=0
    )
    parts = jnp.concatenate([by_rank >> 4, by_rank & 15], axis=0).astype(F32).astype(BF)
    loads[3].wait()
    sender = ones_where(iota((DEVICES, RB), 0) == (kordv[...] ^ me)).astype(BF)
    spread = dot(parts, sender)
    keep = iota((RPB, RB), 0) == (iota((RPB, RB), 1) & (RPB - 1))
    high = jnp.sum(jnp.where(keep, spread[:RPB], 0.0), axis=0, keepdims=True)
    low = jnp.sum(jnp.where(keep, spread[RPB:], 0.0), axis=0, keepdims=True)
    place = (high * 16.0 + low).astype(I32)
    step = RB // CHUNKS
    for n in range(CHUNKS):
        at = place[:, n * step:(n + 1) * step]

        def fill(i, carry):
            mask = (iota((256, step), 0) + i * 256) == at
            placing[n, pl.ds(pl.multiple_of(i * 256, 256), 256), :] = ones_where(mask).astype(BF)
            return carry

        lax.fori_loop(0, RB // 256, fill, 0)

    loads[4].wait()
    pad = jnp.zeros((KR - LEVELS * SLOTS, KR), F32)
    lists = jnp.transpose(jnp.concatenate([skelv[...].astype(F32), pad], axis=0)).astype(I32)
    for j in range(LEVELS):
        for s in range(SLOTS):
            column = lists[:, j * SLOTS + s:j * SLOTS + s + 1]
            mixv[j, s, :, 2 * KR:] = ones_where(iota((KR, 2 * KR), 1) == column).astype(BF)

    lane_slot = iota((KR, WIDE), 1) & (HALF - 1)

    def own_lanes(rows):
        kept = rows[:KR]
        for s in range(1, HALF):
            kept = jnp.where(lane_slot == s, rows[s * KR:(s + 1) * KR], kept)
        return kept

    def exchange(j, g, coeff):
        comb[j, g, :KR, :] = coeff.astype(BF)
        copy = pltpu.make_async_remote_copy(
            comb.at[j, g, pl.ds(0, KR), :], comb.at[j, g, pl.ds(KR, KR), :],
            x_send.at[j, g], x_recv.at[j, g], device_id=(b ^ (1 << j), o), device_id_type=MESH,
        )
        copy.start()
        return copy

    def leaf_step(g):
        total[...] = jnp.zeros_like(total)
        for n in range(CHUNKS):
            rows = step if n < CHUNKS - 1 else step - RPB
            landed = recvb.at[g, pl.ds(n * step, rows), :]
            pltpu.make_async_copy(landed, landed, recv_sem.at[g, n]).wait()
            if n == CHUNKS - 1:
                mine = recvb.at[g, pl.ds(RB - RPB, RPB), :]
                pltpu.make_async_copy(mine, mine, own_sem.at[g]).wait()
            total[...] += dot(placing[n], recvb[g, n * step:(n + 1) * step, :])
        field[...] = total[...].astype(BF)
        products[...] = dot(leafv[g * HALF:(g + 1) * HALF].reshape(HALF * KR, RB), field[...])
        return own_lanes(products[...])

    def level_step(j, g):
        pair = comb[j, g]
        both = jnp.concatenate([pair, pair], axis=0)
        products[...] = dot(mixv[j, g * HALF:(g + 1) * HALF].reshape(HALF * KR, 4 * KR), both)
        return own_lanes(products[...])

    def top_step(g, coeff):
        turned = jnp.transpose(coeff)
        row_slot = iota((WIDE, KR), 0) & (HALF - 1)
        spread_rows = jnp.concatenate(
            [jnp.where(row_slot == s, turned, 0.0).astype(BF) for s in range(HALF)], axis=1
        )
        res = dot_nt(spread_rows, topv[:, g * HALF * KR:(g + 1) * HALF * KR])
        outv[:, g * HALF:(g + 1) * HALF, :] = res.reshape(COLS, HALF, LB)
        copy = pltpu.make_async_copy(
            outv.at[:, pl.ds(g * HALF, HALF), :], out.at[:, pl.ds(g * HALF, HALF), :], out_sem.at[g]
        )
        copy.start()
        return copy

    for copy in loads[5:]:
        copy.wait()
    copies = [[None] * GROUPS for _ in range(LEVELS)]
    for g in range(GROUPS):
        copies[0][g] = exchange(0, g, leaf_step(g))
    coeffs = [None] * GROUPS
    for j in range(LEVELS):
        for g in range(GROUPS):
            copies[j][g].wait()
            coeff = level_step(j, g)
            if j + 1 < LEVELS:
                copies[j + 1][g] = exchange(j + 1, g, coeff)
            else:
                coeffs[g] = coeff.astype(BF).astype(F32)
    stores = [top_step(g, coeffs[g]) for g in range(GROUPS)]
    sent = sendb.at[0, pl.ds(0, OWNERS), :, :]
    for g in range(GROUPS):
        left = recvb.at[g, pl.ds(0, RB - RPB), :]
        pltpu.make_async_copy(left, left, send_sem).wait()
    for copy in stores:
        copy.wait()


def per_device(fourier, cycle_lat, order_table, leaf_op, level_op, skeleton, top_op):
    positions = jnp.repeat(jnp.array(PARTNERS, I32), RPB).reshape(1, RB)
    any_space = pl.BlockSpec(memory_space=pl.ANY)
    dma = pltpu.SemaphoreType.DMA
    return pl.pallas_call(
        kernel,
        out_shape=jax.ShapeDtypeStruct((COLS, SLOTS, LB), F32),
        in_specs=[any_space] * 8,
        out_specs=any_space,
        scratch_shapes=[
            pltpu.VMEM((COLS, ORDERS, ROWS), BF),
            pltpu.VMEM((2 * DEVICES, 128), I32),
            pltpu.VMEM((1, ORDERS), I32),
            pltpu.VMEM((SLOTS, KR, RB), BF),
            pltpu.VMEM((LEVELS, SLOTS, KR, 4 * KR), BF),
            pltpu.VMEM((LEVELS * SLOTS, KR), I32),
            pltpu.VMEM((LB, SLOTS * KR), BF),
            pltpu.VMEM((1, RB), I32),
            pltpu.VMEM((COLS, SLOTS, LB), F32),
            pltpu.VMEM((OWNERS * GROUPS, WIDE, ROWS), F32),
            pltpu.VMEM((GROUPS, OWNERS, ROWS, WIDE), BF),
            pltpu.VMEM((GROUPS, RB, WIDE), BF),
            pltpu.VMEM((CHUNKS, RB, RB // CHUNKS), BF),
            pltpu.VMEM((RB, WIDE), F32),
            pltpu.VMEM((RB, WIDE), BF),
            pltpu.VMEM((HALF * KR, WIDE), F32),
            pltpu.VMEM((LEVELS, GROUPS, 2 * KR, WIDE), BF),
            dma((7 + SLOTS,)),
            dma,
            dma((GROUPS, CHUNKS)),
            dma((GROUPS,)),
            dma((LEVELS, GROUPS)),
            dma((LEVELS, GROUPS)),
            dma((GROUPS,)),
        ],
        compiler_params=pltpu.CompilerParams(
            collective_id=0, has_side_effects=True, vmem_limit_bytes=58 * 1024 * 1024
        ),
    )(
        fourier,
        cycle_lat.reshape(2 * DEVICES, 128),
        order_table.reshape(1, ORDERS),
        leaf_op,
        level_op[:, 0],
        skeleton.reshape(LEVELS * SLOTS, KR),
        top_op,
        positions,
    )


def solution(mesh):
    return jax.shard_map(
        per_device,
        mesh=mesh,
        in_specs=(
            P(None, None, ("blk", "order")),
            P(),
            P(),
            P("order", None, "blk"),
            P(None, "blk", "order", None, None),
            P(None, "blk", "order", None),
            P("order", "blk", None),
        ),
        out_specs=P(None, "order", "blk"),
        check_vma=False,
    )
```

```python
import functools

import jax
import jax.numpy as jnp
import numpy as np
from jax import lax
from jax.experimental import pallas as pl
from jax.experimental.pallas import tpu as pltpu
from jax.sharding import PartitionSpec as P

MESH = pl.DeviceIdType.MESH
BLKS, OWNERS, DEVICES = 16, 8, 128
COLS, ORDERS, ROWS, RPB = 16, 128, 256, 16
SLOTS, HALF, GROUPS = 16, 8, 2
RB, LB, KR, LEVELS = 2048, 1024, 128, 4
RB_SHIFT = 11
WIDE = COLS * HALF
CHUNKS, TAIL, TILE, PART = 8, 2, 256, 256
HEAD = CHUNKS - TAIL
BF, F32, I32 = jnp.bfloat16, jnp.float32, jnp.int32


def hops(k):
    kb, ko = k // OWNERS, k % OWNERS
    z = (kb >> 3) * 2 + (ko >> 2)
    ring = (0, 1, 2, 1)
    return ring[(kb >> 1) & 3] + ring[z] + ring[ko & 3]


PARTNERS = sorted(range(DEVICES), key=lambda k: (-hops(k), (k * 37) % DEVICES))
PARTNERS.remove(0)
PARTNERS.append(0)


ONE, ZERO = np.array(1, BF), np.array(0, BF)


def iota(shape, dim):
    return lax.broadcasted_iota(I32, shape, dim)


def ones_where(mask):
    return jnp.where(mask, 1.0, 0.0).astype(F32)


def dot(a, b):
    return jnp.dot(a, b, preferred_element_type=F32)


def dot_nt(a, b):
    return lax.dot_general(a, b, (((1,), (1,)), ((), ())), preferred_element_type=F32)


def analyse(
    fourier, lat, otab, leaf, level, skel, korder, out,
    fv, latv, otabv, leafv, mixv, skelv, kordv,
    wide, sendb, recvb, placing, turned, total, field, products, comb,
    in_sem, send_sem, recv_sem, own_sem, x_send, x_recv,
):
    b, o = lax.axis_index("blk"), lax.axis_index("order")
    me = b * OWNERS + o

    loads = [
        pltpu.make_async_copy(lat, latv, in_sem.at[0]),
        pltpu.make_async_copy(otab, otabv, in_sem.at[1]),
        pltpu.make_async_copy(fourier, fv, in_sem.at[2]),
        pltpu.make_async_copy(korder, kordv, in_sem.at[3]),
        pltpu.make_async_copy(skel, skelv, in_sem.at[4]),
        pltpu.make_async_copy(leaf, leafv, in_sem.at[5]),
        pltpu.make_async_copy(
            level.at[:, :, :, pl.ds(0, KR)], mixv.at[:, :, :, pl.ds(0, KR)], in_sem.at[6]
        ),
        pltpu.make_async_copy(
            level.at[:, :, :, pl.ds(KR, KR)], mixv.at[:, :, :, pl.ds(2 * KR, KR)], in_sem.at[7]
        ),
    ]
    for copy in loads[:3]:
        copy.start()

    barrier = pltpu.get_barrier_semaphore()
    for k in PARTNERS[:-1]:
        pl.semaphore_signal(
            barrier, inc=1, device_id=(b ^ (k // OWNERS), o ^ (k % OWNERS)), device_id_type=MESH
        )
    for copy in loads[3:]:
        copy.start()

    loads[0].wait()
    own = jnp.concatenate([latv[pl.ds(2 * me, 1), :], latv[pl.ds(2 * me + 1, 1), :]], axis=1)
    own_block = own >> RB_SHIFT
    in_block = ones_where(iota((BLKS, ROWS), 0) == own_block)
    earlier = ones_where(iota((ROWS, ROWS), 0) < iota((ROWS, ROWS), 1)).astype(BF)
    rank = jnp.sum(in_block * dot(in_block.astype(BF), earlier), axis=0, keepdims=True)
    target = own_block * RPB + rank.astype(I32)
    row_pick = ones_where(iota((ROWS, ROWS), 0) == target).astype(BF)

    loads[1].wait()
    order_pick = jnp.transpose(ones_where(iota((ORDERS, ORDERS), 0) == otabv[...])).astype(BF)
    loads[2].wait()
    for c in range(COLS):
        by_slot = dot(order_pick, fv[c])
        wide[:, c * HALF:(c + 1) * HALF, :] = by_slot.reshape(OWNERS * GROUPS, HALF, ROWS)

    def sort_rows(i, carry):
        both = wide[pl.ds(GROUPS * i, GROUPS)].reshape(GROUPS * WIDE, ROWS).astype(BF)
        sendb[i] = dot_nt(row_pick, both).astype(BF)
        return carry

    lax.fori_loop(0, OWNERS, sort_rows, 0)

    def skeleton_step():
        loads[4].wait()
        pad = jnp.zeros((KR - LEVELS * SLOTS, KR), F32)
        lists = jnp.transpose(jnp.concatenate([skelv[...].astype(F32), pad], axis=0)).astype(BF)
        lanes = iota((KR, 2 * KR), 1).astype(F32).astype(BF)
        for j in range(LEVELS):
            for s in range(SLOTS):
                column = lists[:, j * SLOTS + s:j * SLOTS + s + 1]
                chosen = jnp.where(lanes == column, ONE, ZERO)
                mixv[j, s, :, KR:2 * KR] = chosen[:, :KR]
                mixv[j, s, :, 3 * KR:] = chosen[:, KR:]

    def place_step():
        lat_t = jnp.concatenate(
            [jnp.transpose(latv[pl.ds(h, DEVICES, stride=2), :].astype(F32)) for h in range(2)], axis=0
        ).astype(I32)
        here = (lat_t >> RB_SHIFT) == b
        local = lat_t & (RB - 1)
        later = ones_where(iota((ROWS, ROWS), 1) < iota((ROWS, ROWS), 0)).astype(BF)
        ranks = dot(later, ones_where(here).astype(BF)).astype(I32)
        ranks = jnp.where(here, ranks, -1)
        by_rank = jnp.concatenate(
            [jnp.sum(jnp.where(ranks == p, local, 0), axis=0, keepdims=True) for p in range(RPB)], axis=0
        )
        parts = jnp.concatenate([by_rank >> 4, by_rank & 15], axis=0).astype(F32).astype(BF)
        loads[3].wait()
        sender = ones_where(iota((DEVICES, RB), 0) == (kordv[...] ^ me)).astype(BF)
        spread = dot(parts, sender)
        keep = iota((RPB, RB), 0) == (iota((RPB, RB), 1) & (RPB - 1))
        high = jnp.sum(jnp.where(keep, spread[:RPB], 0.0), axis=0, keepdims=True)
        low = jnp.sum(jnp.where(keep, spread[RPB:], 0.0), axis=0, keepdims=True)
        place = high * 16.0 + low
        near = iota((TILE, TILE), 0).astype(F32).astype(BF)
        for n in range(CHUNKS):
            for i in range(RB // TILE):
                at = (place[:, n * TILE:(n + 1) * TILE] - float(i * TILE)).astype(BF)
                placing[n, i * TILE:(i + 1) * TILE, :] = jnp.where(near == at, ONE, ZERO)

    pl.semaphore_wait(barrier, DEVICES - 1)
    for t, k in enumerate(PARTNERS):
        kb, ko = b ^ (k // OWNERS), o ^ (k % OWNERS)
        src = sendb.at[ko, pl.ds(kb * RPB, RPB), :]
        dst = recvb.at[pl.ds(t * RPB, RPB), :]
        if k == 0:
            pltpu.make_async_copy(src, dst, own_sem).start()
        else:
            pltpu.make_async_remote_copy(
                src, dst, send_sem, recv_sem.at[t // (DEVICES // CHUNKS)],
                device_id=(kb, ko), device_id_type=MESH,
            ).start()

    skeleton_step()
    place_step()

    lane_slot = iota((KR, WIDE), 1) & (HALF - 1)

    def own_lanes(rows):
        kept = rows[:KR]
        for s in range(1, HALF):
            kept = jnp.where(lane_slot == s, rows[s * KR:(s + 1) * KR], kept)
        return kept

    def exchange(j, g, coeff):
        comb[j, g, :KR, :] = coeff.astype(BF)
        copy = pltpu.make_async_remote_copy(
            comb.at[j, g, pl.ds(0, KR), :], comb.at[j, g, pl.ds(KR, KR), :],
            x_send.at[j, g], x_recv.at[j, g], device_id=(b ^ (1 << j), o), device_id_type=MESH,
        )
        copy.start()
        return copy

    def slot_rows(ref, g):
        return ref[g * HALF:(g + 1) * HALF].reshape(HALF * KR, ref.shape[2])

    def lanes_of(g):
        return slice(g * WIDE, (g + 1) * WIDE)

    loads[5].wait()
    for i in range(SLOTS // 4):
        some = leafv[4 * i:4 * i + 4].reshape(4 * KR, RB)
        for n in range(TAIL):
            turned[4 * i * KR:4 * (i + 1) * KR, n * TILE:(n + 1) * TILE] = dot(
                some, placing[HEAD + n]
            ).astype(BF)

    def landed(n):
        rows = TILE if n < CHUNKS - 1 else TILE - RPB
        part = recvb.at[pl.ds(n * TILE, rows), :]
        pltpu.make_async_copy(part, part, recv_sem.at[n]).wait()

    for n in range(HEAD):
        landed(n)
        moved = dot(placing[n], recvb[n * TILE:(n + 1) * TILE, :])
        if n == 0:
            total[...] = moved
        elif n < HEAD - 1:
            total[...] += moved
        else:
            field[...] = (total[...] + moved).astype(BF)
    partial = []
    for g in range(GROUPS):
        products[...] = dot(slot_rows(leafv, g), field[:, lanes_of(g)])
        partial.append(own_lanes(products[...]))

    def level_part(j, g, half):
        x = comb[j, g, half * KR:(half + 1) * KR, :]
        rows = slot_rows(mixv.at[j], g)[:, 2 * half * KR:2 * (half + 1) * KR]
        products[...] = dot(rows, jnp.concatenate([x, x], axis=0))
        return own_lanes(products[...])

    for n in range(HEAD, CHUNKS):
        landed(n)
    mine = recvb.at[pl.ds(RB - RPB, RPB), :]
    pltpu.make_async_copy(mine, mine, own_sem).wait()
    copies = [[None] * GROUPS for _ in range(LEVELS)]
    for g in range(GROUPS):
        rows = turned[g * HALF * KR:(g + 1) * HALF * KR, :]
        products[...] = dot(rows, recvb[HEAD * TILE:, lanes_of(g)])
        copies[0][g] = exchange(0, g, partial[g] + own_lanes(products[...]))
    loads[6].wait()
    loads[7].wait()
    for j in range(LEVELS):
        partial = [level_part(j, g, 0) for g in range(GROUPS)]
        for g in range(GROUPS):
            copies[j][g].wait_recv()
            coeff = partial[g] + level_part(j, g, 1)
            if j + 1 < LEVELS:
                copies[j + 1][g] = exchange(j + 1, g, coeff)
            else:
                out[g] = jnp.transpose(coeff).astype(BF)
    for row in copies:
        for copy in row:
            copy.wait_send()
    left = recvb.at[pl.ds(0, RB - RPB), :]
    pltpu.make_async_copy(left, left, send_sem).wait()


def expand(coeff, top, out, block, sem):
    row_slot = iota((WIDE, KR), 0) & (HALF - 1)
    spread = []
    for g in range(GROUPS):
        rows = coeff[g].astype(F32)
        spread.append(jnp.concatenate(
            [jnp.where(row_slot == s, rows, 0.0).astype(BF) for s in range(HALF)], axis=1
        ))
    stores = []
    for n in range(LB // PART):
        at = pl.ds(n * PART, PART)
        for g in range(GROUPS):
            wanted = jnp.concatenate([top[g * HALF + s, at, :] for s in range(HALF)], axis=1)
            block[:, g * HALF:(g + 1) * HALF, at] = dot_nt(spread[g], wanted).reshape(COLS, HALF, PART)
        copy = pltpu.make_async_copy(block.at[:, :, at], out.at[:, :, at], sem.at[n])
        copy.start()
        stores.append(copy)
    for copy in stores:
        copy.wait()


def per_device(fourier, cycle_lat, order_table, leaf_op, level_op, skeleton, top_op):
    positions = jnp.asarray(np.repeat(np.array(PARTNERS, np.int32), RPB).reshape(1, RB))
    hbm = pl.BlockSpec(memory_space=pltpu.HBM)
    dma = pltpu.SemaphoreType.DMA
    coeff = pl.pallas_call(
        analyse,
        out_shape=jax.ShapeDtypeStruct((GROUPS, WIDE, KR), BF),
        in_specs=[hbm] * 7,
        out_specs=pl.BlockSpec(memory_space=pltpu.VMEM),
        scratch_shapes=[
            pltpu.VMEM((COLS, ORDERS, ROWS), BF),
            pltpu.VMEM((2 * DEVICES, 128), I32),
            pltpu.VMEM((1, ORDERS), I32),
            pltpu.VMEM((SLOTS, KR, RB), BF),
            pltpu.VMEM((LEVELS, SLOTS, KR, 4 * KR), BF),
            pltpu.VMEM((LEVELS * SLOTS, KR), I32),
            pltpu.VMEM((1, RB), I32),
            pltpu.VMEM((OWNERS * GROUPS, WIDE, ROWS), F32),
            pltpu.VMEM((OWNERS, ROWS, GROUPS * WIDE), BF),
            pltpu.VMEM((RB, GROUPS * WIDE), BF),
            pltpu.VMEM((CHUNKS, RB, TILE), BF),
            pltpu.VMEM((SLOTS * KR, TAIL * TILE), BF),
            pltpu.VMEM((RB, GROUPS * WIDE), F32),
            pltpu.VMEM((RB, GROUPS * WIDE), BF),
            pltpu.VMEM((HALF * KR, WIDE), F32),
            pltpu.VMEM((LEVELS, GROUPS, 2 * KR, WIDE), BF),
            dma((8,)),
            dma,
            dma((CHUNKS,)),
            dma,
            dma((LEVELS, GROUPS)),
            dma((LEVELS, GROUPS)),
        ],
        compiler_params=pltpu.CompilerParams(
            collective_id=0, has_side_effects=True, vmem_limit_bytes=58 * 1024 * 1024
        ),
    )(
        fourier,
        cycle_lat.reshape(2 * DEVICES, 128),
        order_table.reshape(1, ORDERS),
        leaf_op,
        level_op[:, 0],
        skeleton.reshape(LEVELS * SLOTS, KR),
        positions,
    )
    return pl.pallas_call(
        expand,
        out_shape=jax.ShapeDtypeStruct((COLS, SLOTS, LB), F32),
        in_specs=[pl.BlockSpec(memory_space=pltpu.VMEM)] * 2,
        out_specs=pl.BlockSpec(memory_space=pl.ANY),
        scratch_shapes=[pltpu.VMEM((COLS, SLOTS, LB), F32), dma((LB // PART,))],
        compiler_params=pltpu.CompilerParams(vmem_limit_bytes=16 * 1024 * 1024),
    )(coeff, top_op)


def solution(mesh):
    return jax.shard_map(
        per_device,
        mesh=mesh,
        in_specs=(
            P(None, None, ("blk", "order")),
            P(),
            P(),
            P("order", None, "blk"),
            P(None, "blk", "order", None, None),
            P(None, "blk", "order", None),
            P("order", "blk", None),
        ),
        out_specs=P(None, "order", "blk"),
        check_vma=False,
    )
```

```python
import functools

import jax
import jax.numpy as jnp
import numpy as np
from jax import lax
from jax.experimental import pallas as pl
from jax.experimental.pallas import tpu as pltpu
from jax.sharding import PartitionSpec as P

MESH = pl.DeviceIdType.MESH
BLKS, OWNERS, DEVICES = 16, 8, 128
COLS, ORDERS, ROWS, RPB = 16, 128, 256, 16
SLOTS, HALF, GROUPS = 16, 8, 2
RB, LB, KR, LEVELS = 2048, 1024, 128, 4
RB_SHIFT = 11
WIDE = COLS * HALF
CHUNKS, TAIL, TILE, PART = 8, 2, 256, 256
HEAD = CHUNKS - TAIL
BF, F32, I32 = jnp.bfloat16, jnp.float32, jnp.int32


def hops(k):
    kb, ko = k // OWNERS, k % OWNERS
    z = (kb >> 3) * 2 + (ko >> 2)
    ring = (0, 1, 2, 1)
    return ring[(kb >> 1) & 3] + ring[z] + ring[ko & 3]


FARTHEST = sorted(range(1, DEVICES), key=lambda k: (-hops(k), (k * 37) % DEVICES))
PARTNERS = FARTHEST[:14] + FARTHEST[:13:-1] + [0]


ONE, ZERO = np.array(1, BF), np.array(0, BF)


def iota(shape, dim):
    return lax.broadcasted_iota(I32, shape, dim)


def ones_where(mask):
    return jnp.where(mask, 1.0, 0.0).astype(F32)


def dot(a, b):
    return jnp.dot(a, b, preferred_element_type=F32)


def dot_nt(a, b):
    return lax.dot_general(a, b, (((1,), (1,)), ((), ())), preferred_element_type=F32)


def analyse(
    fourier, lat, otab, leaf, level, skel, korder, out,
    fv, latv, otabv, leafv, mixv, skelv, kordv,
    wide, sendb, recvb, placing, turned, total, field, products, comb,
    in_sem, send_sem, recv_sem, own_sem, x_send, x_recv,
):
    b, o = lax.axis_index("blk"), lax.axis_index("order")
    me = b * OWNERS + o

    loads = [
        pltpu.make_async_copy(lat, latv, in_sem.at[0]),
        pltpu.make_async_copy(otab, otabv, in_sem.at[1]),
        pltpu.make_async_copy(fourier, fv, in_sem.at[2]),
        pltpu.make_async_copy(korder, kordv, in_sem.at[3]),
        pltpu.make_async_copy(skel, skelv, in_sem.at[4]),
        pltpu.make_async_copy(leaf, leafv, in_sem.at[5]),
        pltpu.make_async_copy(
            level.at[:, :, :, pl.ds(0, KR)], mixv.at[:, :, :, pl.ds(0, KR)], in_sem.at[6]
        ),
        pltpu.make_async_copy(
            level.at[:, :, :, pl.ds(KR, KR)], mixv.at[:, :, :, pl.ds(2 * KR, KR)], in_sem.at[7]
        ),
    ]
    for copy in loads[:3]:
        copy.start()

    barrier = pltpu.get_barrier_semaphore()
    for k in FARTHEST:
        pl.semaphore_signal(
            barrier, inc=1, device_id=(b ^ (k // OWNERS), o ^ (k % OWNERS)), device_id_type=MESH
        )
    for copy in loads[3:]:
        copy.start()

    loads[0].wait()
    own = jnp.concatenate([latv[pl.ds(2 * me, 1), :], latv[pl.ds(2 * me + 1, 1), :]], axis=1)
    own_block = own >> RB_SHIFT
    in_block = ones_where(iota((BLKS, ROWS), 0) == own_block)
    earlier = ones_where(iota((ROWS, ROWS), 0) < iota((ROWS, ROWS), 1)).astype(BF)
    rank = jnp.sum(in_block * dot(in_block.astype(BF), earlier), axis=0, keepdims=True)
    target = own_block * RPB + rank.astype(I32)
    row_pick = ones_where(iota((ROWS, ROWS), 0) == target).astype(BF)

    loads[1].wait()
    order_pick = jnp.transpose(ones_where(iota((ORDERS, ORDERS), 0) == otabv[...])).astype(BF)
    loads[2].wait()
    for c in range(COLS):
        by_slot = dot(order_pick, fv[c])
        wide[:, c * HALF:(c + 1) * HALF, :] = by_slot.reshape(OWNERS * GROUPS, HALF, ROWS)

    def sort_rows(i, carry):
        both = wide[pl.ds(GROUPS * i, GROUPS)].reshape(GROUPS * WIDE, ROWS).astype(BF)
        sendb[i] = dot_nt(row_pick, both).astype(BF)
        return carry

    lax.fori_loop(0, OWNERS, sort_rows, 0)

    def skeleton_step():
        loads[4].wait()
        pad = jnp.zeros((KR - LEVELS * SLOTS, KR), F32)
        lists = jnp.transpose(jnp.concatenate([skelv[...].astype(F32), pad], axis=0)).astype(BF)
        lanes = iota((KR, 2 * KR), 1).astype(F32).astype(BF)
        for j in range(LEVELS):
            for s in range(SLOTS):
                column = lists[:, j * SLOTS + s:j * SLOTS + s + 1]
                chosen = jnp.where(lanes == column, ONE, ZERO)
                mixv[j, s, :, KR:2 * KR] = chosen[:, :KR]
                mixv[j, s, :, 3 * KR:] = chosen[:, KR:]

    def place_step():
        lat_t = jnp.concatenate(
            [jnp.transpose(latv[pl.ds(h, DEVICES, stride=2), :].astype(F32)) for h in range(2)], axis=0
        ).astype(I32)
        here = (lat_t >> RB_SHIFT) == b
        local = lat_t & (RB - 1)
        later = ones_where(iota((ROWS, ROWS), 1) < iota((ROWS, ROWS), 0)).astype(BF)
        ranks = dot(later, ones_where(here).astype(BF)).astype(I32)
        ranks = jnp.where(here, ranks, -1)
        by_rank = jnp.concatenate(
            [jnp.sum(jnp.where(ranks == p, local, 0), axis=0, keepdims=True) for p in range(RPB)], axis=0
        )
        parts = jnp.concatenate([by_rank >> 4, by_rank & 15], axis=0).astype(F32).astype(BF)
        loads[3].wait()
        sender = ones_where(iota((DEVICES, RB), 0) == (kordv[...] ^ me)).astype(BF)
        spread = dot(parts, sender)
        keep = iota((RPB, RB), 0) == (iota((RPB, RB), 1) & (RPB - 1))
        high = jnp.sum(jnp.where(keep, spread[:RPB], 0.0), axis=0, keepdims=True)
        low = jnp.sum(jnp.where(keep, spread[RPB:], 0.0), axis=0, keepdims=True)
        place = high * 16.0 + low
        near = iota((TILE, TILE), 0).astype(F32).astype(BF)
        for n in range(CHUNKS):
            for i in range(RB // TILE):
                at = (place[:, n * TILE:(n + 1) * TILE] - float(i * TILE)).astype(BF)
                placing[n, i * TILE:(i + 1) * TILE, :] = jnp.where(near == at, ONE, ZERO)

    pl.semaphore_wait(barrier, DEVICES - 1)
    for t, k in enumerate(PARTNERS):
        kb, ko = b ^ (k // OWNERS), o ^ (k % OWNERS)
        src = sendb.at[ko, pl.ds(kb * RPB, RPB), :]
        dst = recvb.at[pl.ds(t * RPB, RPB), :]
        if k == 0:
            pltpu.make_async_copy(src, dst, own_sem).start()
        else:
            pltpu.make_async_remote_copy(
                src, dst, send_sem, recv_sem.at[t // (DEVICES // CHUNKS)],
                device_id=(kb, ko), device_id_type=MESH,
            ).start()

    skeleton_step()
    place_step()

    lane_slot = iota((KR, WIDE), 1) & (HALF - 1)

    def own_lanes(rows):
        kept = rows[:KR]
        for s in range(1, HALF):
            kept = jnp.where(lane_slot == s, rows[s * KR:(s + 1) * KR], kept)
        return kept

    def exchange(j, g, coeff):
        comb[j, g, :KR, :] = coeff.astype(BF)
        copy = pltpu.make_async_remote_copy(
            comb.at[j, g, pl.ds(0, KR), :], comb.at[j, g, pl.ds(KR, KR), :],
            x_send.at[j, g], x_recv.at[j, g], device_id=(b ^ (1 << j), o), device_id_type=MESH,
        )
        copy.start()
        return copy

    def slot_rows(ref, g):
        return ref[g * HALF:(g + 1) * HALF].reshape(HALF * KR, ref.shape[2])

    def lanes_of(g):
        return slice(g * WIDE, (g + 1) * WIDE)

    loads[5].wait()
    for i in range(SLOTS // 4):
        some = leafv[4 * i:4 * i + 4].reshape(4 * KR, RB)
        for n in range(TAIL):
            turned[4 * i * KR:4 * (i + 1) * KR, n * TILE:(n + 1) * TILE] = dot(
                some, placing[HEAD + n]
            ).astype(BF)

    def landed(n):
        rows = TILE if n < CHUNKS - 1 else TILE - RPB
        part = recvb.at[pl.ds(n * TILE, rows), :]
        pltpu.make_async_copy(part, part, recv_sem.at[n]).wait()

    for n in range(HEAD):
        landed(n)
        moved = dot(placing[n], recvb[n * TILE:(n + 1) * TILE, :])
        if n == 0:
            total[...] = moved
        elif n < HEAD - 1:
            total[...] += moved
        else:
            field[...] = (total[...] + moved).astype(BF)
    partial = []
    for g in range(GROUPS):
        products[...] = dot(slot_rows(leafv, g), field[:, lanes_of(g)])
        partial.append(own_lanes(products[...]))

    def level_part(j, g, half):
        x = comb[j, g, half * KR:(half + 1) * KR, :]
        rows = slot_rows(mixv.at[j], g)[:, 2 * half * KR:2 * (half + 1) * KR]
        products[...] = dot(rows, jnp.concatenate([x, x], axis=0))
        return own_lanes(products[...])

    for n in range(HEAD, CHUNKS):
        landed(n)
    mine = recvb.at[pl.ds(RB - RPB, RPB), :]
    pltpu.make_async_copy(mine, mine, own_sem).wait()
    copies = [[None] * GROUPS for _ in range(LEVELS)]
    for g in range(GROUPS):
        rows = turned[g * HALF * KR:(g + 1) * HALF * KR, :]
        products[...] = dot(rows, recvb[HEAD * TILE:, lanes_of(g)])
        copies[0][g] = exchange(0, g, partial[g] + own_lanes(products[...]))
    loads[6].wait()
    loads[7].wait()
    for j in range(LEVELS):
        partial = [level_part(j, g, 0) for g in range(GROUPS)]
        for g in range(GROUPS):
            copies[j][g].wait_recv()
            coeff = partial[g] + level_part(j, g, 1)
            if j + 1 < LEVELS:
                copies[j + 1][g] = exchange(j + 1, g, coeff)
            else:
                out[g] = jnp.transpose(coeff).astype(BF)
    for row in copies:
        for copy in row:
            copy.wait_send()
    left = recvb.at[pl.ds(0, RB - RPB), :]
    pltpu.make_async_copy(left, left, send_sem).wait()


def expand(coeff, top, out, block, sem):
    row_slot = iota((WIDE, KR), 0) & (HALF - 1)
    spread = []
    for g in range(GROUPS):
        rows = coeff[g].astype(F32)
        spread.append(jnp.concatenate(
            [jnp.where(row_slot == s, rows, 0.0).astype(BF) for s in range(HALF)], axis=1
        ))
    stores = []
    for n in range(LB // PART):
        at = pl.ds(n * PART, PART)
        for g in range(GROUPS):
            wanted = jnp.concatenate([top[g * HALF + s, at, :] for s in range(HALF)], axis=1)
            block[:, g * HALF:(g + 1) * HALF, at] = dot_nt(spread[g], wanted).reshape(COLS, HALF, PART)
        copy = pltpu.make_async_copy(block.at[:, :, at], out.at[:, :, at], sem.at[n])
        copy.start()
        stores.append(copy)
    for copy in stores:
        copy.wait()


def per_device(fourier, cycle_lat, order_table, leaf_op, level_op, skeleton, top_op):
    positions = jnp.asarray(np.repeat(np.array(PARTNERS, np.int32), RPB).reshape(1, RB))
    hbm = pl.BlockSpec(memory_space=pltpu.HBM)
    dma = pltpu.SemaphoreType.DMA
    coeff = pl.pallas_call(
        analyse,
        out_shape=jax.ShapeDtypeStruct((GROUPS, WIDE, KR), BF),
        in_specs=[hbm] * 7,
        out_specs=pl.BlockSpec(memory_space=pltpu.VMEM),
        scratch_shapes=[
            pltpu.VMEM((COLS, ORDERS, ROWS), BF),
            pltpu.VMEM((2 * DEVICES, 128), I32),
            pltpu.VMEM((1, ORDERS), I32),
            pltpu.VMEM((SLOTS, KR, RB), BF),
            pltpu.VMEM((LEVELS, SLOTS, KR, 4 * KR), BF),
            pltpu.VMEM((LEVELS * SLOTS, KR), I32),
            pltpu.VMEM((1, RB), I32),
            pltpu.VMEM((OWNERS * GROUPS, WIDE, ROWS), F32),
            pltpu.VMEM((OWNERS, ROWS, GROUPS * WIDE), BF),
            pltpu.VMEM((RB, GROUPS * WIDE), BF),
            pltpu.VMEM((CHUNKS, RB, TILE), BF),
            pltpu.VMEM((SLOTS * KR, TAIL * TILE), BF),
            pltpu.VMEM((RB, GROUPS * WIDE), F32),
            pltpu.VMEM((RB, GROUPS * WIDE), BF),
            pltpu.VMEM((HALF * KR, WIDE), F32),
            pltpu.VMEM((LEVELS, GROUPS, 2 * KR, WIDE), BF),
            dma((8,)),
            dma,
            dma((CHUNKS,)),
            dma,
            dma((LEVELS, GROUPS)),
            dma((LEVELS, GROUPS)),
        ],
        compiler_params=pltpu.CompilerParams(
            collective_id=0, has_side_effects=True, vmem_limit_bytes=50 * 1024 * 1024
        ),
    )(*(
        pltpu.with_memory_space_constraint(x, pltpu.HBM)
        for x in (
            fourier,
            cycle_lat.reshape(2 * DEVICES, 128),
            order_table.reshape(1, ORDERS),
            leaf_op,
            level_op[:, 0],
            skeleton.reshape(LEVELS * SLOTS, KR),
            positions,
        )
    ))
    return pl.pallas_call(
        expand,
        out_shape=jax.ShapeDtypeStruct((COLS, SLOTS, LB), F32),
        in_specs=[pl.BlockSpec(memory_space=pltpu.VMEM)] * 2,
        out_specs=pl.BlockSpec(memory_space=pl.ANY),
        scratch_shapes=[pltpu.VMEM((COLS, SLOTS, LB), F32), dma((LB // PART,))],
        compiler_params=pltpu.CompilerParams(vmem_limit_bytes=16 * 1024 * 1024),
    )(coeff, top_op)


def solution(mesh):
    return jax.shard_map(
        per_device,
        mesh=mesh,
        in_specs=(
            P(None, None, ("blk", "order")),
            P(),
            P(),
            P("order", None, "blk"),
            P(None, "blk", "order", None, None),
            P(None, "blk", "order", None),
            P("order", "blk", None),
        ),
        out_specs=P(None, "order", "blk"),
        check_vma=False,
    )
```

```python
import functools

import jax
import jax.numpy as jnp
import numpy as np
from jax import lax
from jax.experimental import pallas as pl
from jax.experimental.pallas import tpu as pltpu
from jax.sharding import PartitionSpec as P

MESH = pl.DeviceIdType.MESH
BLKS, OWNERS, DEVICES = 16, 8, 128
COLS, ORDERS, ROWS, RPB = 16, 128, 256, 16
SLOTS, HALF, GROUPS = 16, 8, 2
RB, LB, KR, LEVELS = 2048, 1024, 128, 4
RB_SHIFT = 11
WIDE = COLS * HALF
CHUNKS, TAIL, TILE, PART = 8, 2, 256, 256
HEAD = CHUNKS - TAIL
BF, F32, I32 = jnp.bfloat16, jnp.float32, jnp.int32


def hops(k):
    kb, ko = k // OWNERS, k % OWNERS
    z = (kb >> 3) * 2 + (ko >> 2)
    ring = (0, 1, 2, 1)
    return ring[(kb >> 1) & 3] + ring[z] + ring[ko & 3]


FARTHEST = sorted(range(1, DEVICES), key=lambda k: (-hops(k), (k * 37) % DEVICES))
PARTNERS = FARTHEST[:14] + FARTHEST[:13:-1] + [0]


ONE, ZERO = np.array(1, BF), np.array(0, BF)


def iota(shape, dim):
    return lax.broadcasted_iota(I32, shape, dim)


def ones_where(mask):
    return jnp.where(mask, 1.0, 0.0).astype(F32)


def dot(a, b):
    return jnp.dot(a, b, preferred_element_type=F32)


def dot_nt(a, b):
    return lax.dot_general(a, b, (((1,), (1,)), ((), ())), preferred_element_type=F32)


def analyse(
    fourier, lat, otab, leaf, level, skel, korder, top, out, top_out,
    topv, fv, latv, otabv, leafv, mixv, skelv, kordv,
    wide, sendb, recvb, placing, turned, total, field, comb,
    in_sem, send_sem, recv_sem, own_sem, x_send, x_recv,
):
    b, o = lax.axis_index("blk"), lax.axis_index("order")
    me = b * OWNERS + o

    loads = [
        pltpu.make_async_copy(lat, latv, in_sem.at[0]),
        pltpu.make_async_copy(otab, otabv, in_sem.at[1]),
        pltpu.make_async_copy(fourier, fv, in_sem.at[2]),
        pltpu.make_async_copy(korder, kordv, in_sem.at[3]),
        pltpu.make_async_copy(skel, skelv, in_sem.at[4]),
        pltpu.make_async_copy(leaf, leafv, in_sem.at[5]),
        pltpu.make_async_copy(
            level.at[:, :, :, pl.ds(0, KR)], mixv.at[:, :, :, pl.ds(0, KR)], in_sem.at[6]
        ),
        pltpu.make_async_copy(
            level.at[:, :, :, pl.ds(KR, KR)], mixv.at[:, :, :, pl.ds(2 * KR, KR)], in_sem.at[7]
        ),
        pltpu.make_async_copy(top, topv, in_sem.at[8]),
    ]
    for copy in loads[:3]:
        copy.start()

    barrier = pltpu.get_barrier_semaphore()
    for k in FARTHEST:
        pl.semaphore_signal(
            barrier, inc=1, device_id=(b ^ (k // OWNERS), o ^ (k % OWNERS)), device_id_type=MESH
        )
    for copy in loads[3:]:
        copy.start()

    loads[0].wait()
    own = jnp.concatenate([latv[pl.ds(2 * me, 1), :], latv[pl.ds(2 * me + 1, 1), :]], axis=1)
    own_block = own >> RB_SHIFT
    in_block = ones_where(iota((BLKS, ROWS), 0) == own_block)
    earlier = ones_where(iota((ROWS, ROWS), 0) < iota((ROWS, ROWS), 1)).astype(BF)
    rank = jnp.sum(in_block * dot(in_block.astype(BF), earlier), axis=0, keepdims=True)
    target = own_block * RPB + rank.astype(I32)
    row_pick = ones_where(iota((ROWS, ROWS), 0) == target).astype(BF)

    loads[1].wait()
    order_pick = jnp.transpose(ones_where(iota((ORDERS, ORDERS), 0) == otabv[...])).astype(BF)
    loads[2].wait()
    for c in range(COLS):
        by_slot = dot(order_pick, fv[c])
        wide[:, c * HALF:(c + 1) * HALF, :] = by_slot.reshape(OWNERS * GROUPS, HALF, ROWS)

    def sort_rows(i, carry):
        both = wide[pl.ds(GROUPS * i, GROUPS)].reshape(GROUPS * WIDE, ROWS).astype(BF)
        sendb[i] = dot_nt(row_pick, both).astype(BF)
        return carry

    lax.fori_loop(0, OWNERS, sort_rows, 0)

    def skeleton_step():
        loads[4].wait()
        pad = jnp.zeros((KR - LEVELS * SLOTS, KR), F32)
        lists = jnp.transpose(jnp.concatenate([skelv[...].astype(F32), pad], axis=0)).astype(BF)
        lanes = iota((KR, 2 * KR), 1).astype(F32).astype(BF)
        for j in range(LEVELS):
            for s in range(SLOTS):
                column = lists[:, j * SLOTS + s:j * SLOTS + s + 1]
                chosen = jnp.where(lanes == column, ONE, ZERO)
                mixv[j, s, :, KR:2 * KR] = chosen[:, :KR]
                mixv[j, s, :, 3 * KR:] = chosen[:, KR:]

    def place_step():
        lat_t = jnp.concatenate(
            [jnp.transpose(latv[pl.ds(h, DEVICES, stride=2), :].astype(F32)) for h in range(2)], axis=0
        ).astype(I32)
        here = (lat_t >> RB_SHIFT) == b
        local = lat_t & (RB - 1)
        later = ones_where(iota((ROWS, ROWS), 1) < iota((ROWS, ROWS), 0)).astype(BF)
        ranks = dot(later, ones_where(here).astype(BF)).astype(I32)
        ranks = jnp.where(here, ranks, -1)
        by_rank = jnp.concatenate(
            [jnp.sum(jnp.where(ranks == p, local, 0), axis=0, keepdims=True) for p in range(RPB)], axis=0
        )
        parts = jnp.concatenate([by_rank >> 4, by_rank & 15], axis=0).astype(F32).astype(BF)
        loads[3].wait()
        sender = ones_where(iota((DEVICES, RB), 0) == (kordv[...] ^ me)).astype(BF)
        spread = dot(parts, sender)
        keep = iota((RPB, RB), 0) == (iota((RPB, RB), 1) & (RPB - 1))
        high = jnp.sum(jnp.where(keep, spread[:RPB], 0.0), axis=0, keepdims=True)
        low = jnp.sum(jnp.where(keep, spread[RPB:], 0.0), axis=0, keepdims=True)
        place = high * 16.0 + low
        near = iota((TILE, TILE), 0).astype(F32).astype(BF)
        for n in range(CHUNKS):
            for i in range(RB // TILE):
                at = (place[:, n * TILE:(n + 1) * TILE] - float(i * TILE)).astype(BF)
                placing[n, i * TILE:(i + 1) * TILE, :] = jnp.where(near == at, ONE, ZERO)

    pl.semaphore_wait(barrier, DEVICES - 1)
    for t, k in enumerate(PARTNERS):
        kb, ko = b ^ (k // OWNERS), o ^ (k % OWNERS)
        src = sendb.at[ko, pl.ds(kb * RPB, RPB), :]
        dst = recvb.at[pl.ds(t * RPB, RPB), :]
        if k == 0:
            pltpu.make_async_copy(src, dst, own_sem).start()
        else:
            pltpu.make_async_remote_copy(
                src, dst, send_sem, recv_sem.at[t // (DEVICES // CHUNKS)],
                device_id=(kb, ko), device_id_type=MESH,
            ).start()

    skeleton_step()
    place_step()

    lane_slot = iota((KR, WIDE), 1) & (HALF - 1)

    def own_lanes(rows_of, x):
        kept = dot(rows_of(0), x)
        for s in range(1, HALF):
            kept = jnp.where(lane_slot == s, dot(rows_of(s), x), kept)
        return kept

    def exchange(j, g, coeff):
        comb[j, g, :KR, :] = coeff.astype(BF)
        copy = pltpu.make_async_remote_copy(
            comb.at[j, g, pl.ds(0, KR), :], comb.at[j, g, pl.ds(KR, KR), :],
            x_send.at[j, g], x_recv.at[j, g], device_id=(b ^ (1 << j), o), device_id_type=MESH,
        )
        copy.start()
        return copy

    def lanes_of(g):
        return slice(g * WIDE, (g + 1) * WIDE)

    loads[5].wait()
    for i in range(SLOTS // 4):
        some = leafv[4 * i:4 * i + 4].reshape(4 * KR, RB)
        for n in range(TAIL):
            turned[4 * i * KR:4 * (i + 1) * KR, n * TILE:(n + 1) * TILE] = dot(
                some, placing[HEAD + n]
            ).astype(BF)

    loads[8].wait()
    eye = ones_where(iota((TILE, TILE), 0) == iota((TILE, TILE), 1)).astype(BF)
    for pair in range(SLOTS // 2):
        for i in range(LB // PART):
            at = slice(i * PART, (i + 1) * PART)
            both = jnp.concatenate([topv[2 * pair, at, :], topv[2 * pair + 1, at, :]], axis=1)
            top_out[pair * 2 * KR:(pair + 1) * 2 * KR, at] = dot_nt(eye, both).astype(BF)

    def landed(n):
        rows = TILE if n < CHUNKS - 1 else TILE - RPB
        part = recvb.at[pl.ds(n * TILE, rows), :]
        pltpu.make_async_copy(part, part, recv_sem.at[n]).wait()

    for n in range(HEAD):
        landed(n)
        moved = dot(placing[n], recvb[n * TILE:(n + 1) * TILE, :])
        if n == 0:
            total[...] = moved
        elif n < HEAD - 1:
            total[...] += moved
        else:
            field[...] = (total[...] + moved).astype(BF)
    partial = []
    for g in range(GROUPS):
        partial.append(own_lanes(lambda s: leafv[g * HALF + s], field[:, lanes_of(g)]))

    def level_part(j, g, half):
        x = comb[j, g, half * KR:(half + 1) * KR, :]
        part = slice(2 * half * KR, 2 * (half + 1) * KR)
        return own_lanes(lambda s: mixv[j, g * HALF + s, :, part], jnp.concatenate([x, x], axis=0))

    for n in range(HEAD, CHUNKS):
        landed(n)
    mine = recvb.at[pl.ds(RB - RPB, RPB), :]
    pltpu.make_async_copy(mine, mine, own_sem).wait()
    copies = [[None] * GROUPS for _ in range(LEVELS)]
    for g in range(GROUPS):
        rest = own_lanes(
            lambda s: turned[(g * HALF + s) * KR:(g * HALF + s + 1) * KR, :], recvb[HEAD * TILE:, lanes_of(g)]
        )
        copies[0][g] = exchange(0, g, partial[g] + rest)
    loads[6].wait()
    loads[7].wait()
    for j in range(LEVELS):
        partial = [level_part(j, g, 0) for g in range(GROUPS)]
        for g in range(GROUPS):
            copies[j][g].wait_recv()
            coeff = partial[g] + level_part(j, g, 1)
            if j + 1 < LEVELS:
                copies[j + 1][g] = exchange(j + 1, g, coeff)
            else:
                out[g] = jnp.transpose(coeff).astype(BF)
    for row in copies:
        for copy in row:
            copy.wait_send()
    left = recvb.at[pl.ds(0, RB - RPB), :]
    pltpu.make_async_copy(left, left, send_sem).wait()


def expand(coeff, top, out, block, sem):
    row_slot = iota((WIDE, KR), 0) & (HALF - 1)
    spread = []
    for g in range(GROUPS):
        rows = coeff[g].astype(F32)
        spread.append(jnp.concatenate(
            [jnp.where(row_slot == s, rows, 0.0).astype(BF) for s in range(HALF)], axis=1
        ))
    stores = []
    for n in range(LB // PART):
        at = pl.ds(n * PART, PART)
        for g in range(GROUPS):
            wanted = top[g * HALF * KR:(g + 1) * HALF * KR, at]
            block[:, g * HALF:(g + 1) * HALF, at] = dot(spread[g], wanted).reshape(COLS, HALF, PART)
        copy = pltpu.make_async_copy(block.at[:, :, at], out.at[:, :, at], sem.at[n])
        copy.start()
        stores.append(copy)
    for copy in stores:
        copy.wait()


def per_device(fourier, cycle_lat, order_table, leaf_op, level_op, skeleton, top_op):
    positions = jnp.asarray(np.repeat(np.array(PARTNERS, np.int32), RPB).reshape(1, RB))
    hbm = pl.BlockSpec(memory_space=pltpu.HBM)
    dma = pltpu.SemaphoreType.DMA
    coeff, top_turned = pl.pallas_call(
        analyse,
        out_shape=(
            jax.ShapeDtypeStruct((GROUPS, WIDE, KR), BF),
            jax.ShapeDtypeStruct((SLOTS * KR, LB), BF),
        ),
        in_specs=[hbm] * 8,
        out_specs=[pl.BlockSpec(memory_space=pltpu.VMEM)] * 2,
        scratch_shapes=[
            pltpu.VMEM((SLOTS, LB, KR), BF),
            pltpu.VMEM((COLS, ORDERS, ROWS), BF),
            pltpu.VMEM((2 * DEVICES, 128), I32),
            pltpu.VMEM((1, ORDERS), I32),
            pltpu.VMEM((SLOTS, KR, RB), BF),
            pltpu.VMEM((LEVELS, SLOTS, KR, 4 * KR), BF),
            pltpu.VMEM((LEVELS * SLOTS, KR), I32),
            pltpu.VMEM((1, RB), I32),
            pltpu.VMEM((OWNERS * GROUPS, WIDE, ROWS), F32),
            pltpu.VMEM((OWNERS, ROWS, GROUPS * WIDE), BF),
            pltpu.VMEM((RB, GROUPS * WIDE), BF),
            pltpu.VMEM((CHUNKS, RB, TILE), BF),
            pltpu.VMEM((SLOTS * KR, TAIL * TILE), BF),
            pltpu.VMEM((RB, GROUPS * WIDE), F32),
            pltpu.VMEM((RB, GROUPS * WIDE), BF),
            pltpu.VMEM((LEVELS, GROUPS, 2 * KR, WIDE), BF),
            dma((9,)),
            dma,
            dma((CHUNKS,)),
            dma,
            dma((LEVELS, GROUPS)),
            dma((LEVELS, GROUPS)),
        ],
        compiler_params=pltpu.CompilerParams(
            collective_id=0, has_side_effects=True, vmem_limit_bytes=44 * 1024 * 1024
        ),
    )(*(
        pltpu.with_memory_space_constraint(x, pltpu.HBM)
        for x in (
            fourier,
            cycle_lat.reshape(2 * DEVICES, 128),
            order_table.reshape(1, ORDERS),
            leaf_op,
            level_op[:, 0],
            skeleton.reshape(LEVELS * SLOTS, KR),
            positions,
            top_op,
        )
    ))
    return pl.pallas_call(
        expand,
        out_shape=jax.ShapeDtypeStruct((COLS, SLOTS, LB), F32),
        in_specs=[pl.BlockSpec(memory_space=pltpu.VMEM)] * 2,
        out_specs=pl.BlockSpec(memory_space=pl.ANY),
        scratch_shapes=[pltpu.VMEM((COLS, SLOTS, LB), F32), dma((LB // PART,))],
        compiler_params=pltpu.CompilerParams(vmem_limit_bytes=16 * 1024 * 1024),
    )(coeff, top_turned)


def solution(mesh):
    return jax.shard_map(
        per_device,
        mesh=mesh,
        in_specs=(
            P(None, None, ("blk", "order")),
            P(),
            P(),
            P("order", None, "blk"),
            P(None, "blk", "order", None, None),
            P(None, "blk", "order", None),
            P("order", "blk", None),
        ),
        out_specs=P(None, "order", "blk"),
        check_vma=False,
    )
```

```python
import functools

import jax
import jax.numpy as jnp
import numpy as np
from jax import lax
from jax.experimental import pallas as pl
from jax.experimental.pallas import tpu as pltpu
from jax.sharding import PartitionSpec as P

MESH = pl.DeviceIdType.MESH
BLKS, OWNERS, DEVICES = 16, 8, 128
COLS, ORDERS, ROWS, RPB = 16, 128, 256, 16
SLOTS, HALF, GROUPS = 16, 8, 2
RB, LB, KR, LEVELS = 2048, 1024, 128, 4
RB_SHIFT = 11
WIDE = COLS * HALF
CHUNKS, TAIL, TILE, PART = 8, 2, 256, 256
HEAD = CHUNKS - TAIL
BF, F32, I32 = jnp.bfloat16, jnp.float32, jnp.int32


def hops(k):
    kb, ko = k // OWNERS, k % OWNERS
    z = (kb >> 3) * 2 + (ko >> 2)
    ring = (0, 1, 2, 1)
    return ring[(kb >> 1) & 3] + ring[z] + ring[ko & 3]


FARTHEST = sorted(range(1, DEVICES), key=lambda k: (-hops(k), (k * 37) % DEVICES))
PARTNERS = FARTHEST[:14] + FARTHEST[:13:-1] + [0]


ONE, ZERO = np.array(1, BF), np.array(0, BF)


def iota(shape, dim):
    return lax.broadcasted_iota(I32, shape, dim)


def ones_where(mask):
    return jnp.where(mask, 1.0, 0.0).astype(F32)


def dot(a, b):
    return jnp.dot(a, b, preferred_element_type=F32)


def dot_nt(a, b):
    return lax.dot_general(a, b, (((1,), (1,)), ((), ())), preferred_element_type=F32)


def analyse(
    fourier, lat, otab, leaf, level, skel, korder, top, out, top_out,
    topv, fv, latv, otabv, leafv, mixv, skelv, kordv,
    wide, sendb, recvb, placing, turned, total, field, comb,
    in_sem, send_sem, recv_sem, own_sem, x_send, x_recv,
):
    b, o = lax.axis_index("blk"), lax.axis_index("order")
    me = b * OWNERS + o

    loads = [
        pltpu.make_async_copy(lat, latv, in_sem.at[0]),
        pltpu.make_async_copy(otab, otabv, in_sem.at[1]),
        pltpu.make_async_copy(fourier, fv, in_sem.at[2]),
        pltpu.make_async_copy(korder, kordv, in_sem.at[3]),
        pltpu.make_async_copy(skel, skelv, in_sem.at[4]),
        pltpu.make_async_copy(leaf, leafv, in_sem.at[5]),
        pltpu.make_async_copy(
            level.at[:, :, :, pl.ds(0, KR)], mixv.at[:, :, :, pl.ds(0, KR)], in_sem.at[6]
        ),
        pltpu.make_async_copy(
            level.at[:, :, :, pl.ds(KR, KR)], mixv.at[:, :, :, pl.ds(2 * KR, KR)], in_sem.at[7]
        ),
        pltpu.make_async_copy(top, topv, in_sem.at[8]),
    ]
    for copy in loads[:3]:
        copy.start()

    barrier = pltpu.get_barrier_semaphore()
    for k in FARTHEST:
        pl.semaphore_signal(
            barrier, inc=1, device_id=(b ^ (k // OWNERS), o ^ (k % OWNERS)), device_id_type=MESH
        )
    for copy in loads[3:]:
        copy.start()

    loads[0].wait()
    own = jnp.concatenate([latv[pl.ds(2 * me, 1), :], latv[pl.ds(2 * me + 1, 1), :]], axis=1)
    own_block = own >> RB_SHIFT
    in_block = ones_where(iota((BLKS, ROWS), 0) == own_block)
    earlier = ones_where(iota((ROWS, ROWS), 0) < iota((ROWS, ROWS), 1)).astype(BF)
    rank = jnp.sum(in_block * dot(in_block.astype(BF), earlier), axis=0, keepdims=True)
    target = own_block * RPB + rank.astype(I32)
    row_pick = ones_where(iota((ROWS, ROWS), 0) == target).astype(BF)

    loads[1].wait()
    order_pick = jnp.transpose(ones_where(iota((ORDERS, ORDERS), 0) == otabv[...])).astype(BF)
    loads[2].wait()
    for c in range(COLS):
        by_slot = dot(order_pick, fv[c])
        wide[:, c * HALF:(c + 1) * HALF, :] = by_slot.reshape(OWNERS * GROUPS, HALF, ROWS)

    def sort_rows(i, carry):
        both = wide[pl.ds(GROUPS * i, GROUPS)].reshape(GROUPS * WIDE, ROWS).astype(BF)
        sendb[i] = dot_nt(row_pick, both).astype(BF)
        return carry

    lax.fori_loop(0, OWNERS, sort_rows, 0)

    def skeleton_step():
        loads[4].wait()
        pad = jnp.zeros((KR - LEVELS * SLOTS, KR), F32)
        lists = jnp.transpose(jnp.concatenate([skelv[...].astype(F32), pad], axis=0)).astype(BF)
        lanes = iota((KR, 2 * KR), 1).astype(F32).astype(BF)
        for j in range(LEVELS):
            for s in range(SLOTS):
                column = lists[:, j * SLOTS + s:j * SLOTS + s + 1]
                chosen = jnp.where(lanes == column, ONE, ZERO)
                mixv[j, s, :, KR:2 * KR] = chosen[:, :KR]
                mixv[j, s, :, 3 * KR:] = chosen[:, KR:]

    def place_step():
        lat_t = jnp.concatenate(
            [jnp.transpose(latv[pl.ds(h, DEVICES, stride=2), :].astype(F32)) for h in range(2)], axis=0
        ).astype(I32)
        here = (lat_t >> RB_SHIFT) == b
        local = lat_t & (RB - 1)
        later = ones_where(iota((ROWS, ROWS), 1) < iota((ROWS, ROWS), 0)).astype(BF)
        ranks = dot(later, ones_where(here).astype(BF)).astype(I32)
        ranks = jnp.where(here, ranks, -1)
        by_rank = jnp.concatenate(
            [jnp.sum(jnp.where(ranks == p, local, 0), axis=0, keepdims=True) for p in range(RPB)], axis=0
        )
        parts = jnp.concatenate([by_rank >> 4, by_rank & 15], axis=0).astype(F32).astype(BF)
        loads[3].wait()
        sender = ones_where(iota((DEVICES, RB), 0) == (kordv[...] ^ me)).astype(BF)
        spread = dot(parts, sender)
        keep = iota((RPB, RB), 0) == (iota((RPB, RB), 1) & (RPB - 1))
        high = jnp.sum(jnp.where(keep, spread[:RPB], 0.0), axis=0, keepdims=True)
        low = jnp.sum(jnp.where(keep, spread[RPB:], 0.0), axis=0, keepdims=True)
        place = high * 16.0 + low
        near = iota((TILE, TILE), 0).astype(F32).astype(BF)
        for n in range(CHUNKS):
            for i in range(RB // TILE):
                at = (place[:, n * TILE:(n + 1) * TILE] - float(i * TILE)).astype(BF)
                placing[n, i * TILE:(i + 1) * TILE, :] = jnp.where(near == at, ONE, ZERO)

    pl.semaphore_wait(barrier, DEVICES - 1)
    for t, k in enumerate(PARTNERS):
        kb, ko = b ^ (k // OWNERS), o ^ (k % OWNERS)
        src = sendb.at[ko, pl.ds(kb * RPB, RPB), :]
        dst = recvb.at[pl.ds(t * RPB, RPB), :]
        if k == 0:
            pltpu.make_async_copy(src, dst, own_sem).start()
        else:
            pltpu.make_async_remote_copy(
                src, dst, send_sem, recv_sem.at[t // (DEVICES // CHUNKS)],
                device_id=(kb, ko), device_id_type=MESH,
            ).start()

    skeleton_step()
    place_step()

    lane_slot = iota((KR, WIDE), 1) & (HALF - 1)

    def own_lanes(rows_of, x):
        kept = dot(rows_of(0), x)
        for s in range(1, HALF):
            kept = jnp.where(lane_slot == s, dot(rows_of(s), x), kept)
        return kept

    def exchange(j, g, coeff):
        comb[j, g, :KR, :] = coeff.astype(BF)
        copy = pltpu.make_async_remote_copy(
            comb.at[j, g, pl.ds(0, KR), :], comb.at[j, g, pl.ds(KR, KR), :],
            x_send.at[j, g], x_recv.at[j, g], device_id=(b ^ (1 << j), o), device_id_type=MESH,
        )
        copy.start()
        return copy

    def lanes_of(g):
        return slice(g * WIDE, (g + 1) * WIDE)

    loads[5].wait()
    for i in range(SLOTS // 4):
        some = leafv[4 * i:4 * i + 4].reshape(4 * KR, RB)
        for n in range(TAIL):
            turned[4 * i * KR:4 * (i + 1) * KR, n * TILE:(n + 1) * TILE] = dot(
                some, placing[HEAD + n]
            ).astype(BF)

    loads[8].wait()
    eye = ones_where(iota((TILE, TILE), 0) == iota((TILE, TILE), 1)).astype(BF)
    for pair in range(SLOTS // 2):
        for i in range(LB // PART):
            at = slice(i * PART, (i + 1) * PART)
            both = jnp.concatenate([topv[2 * pair, at, :], topv[2 * pair + 1, at, :]], axis=1)
            top_out[pair * 2 * KR:(pair + 1) * 2 * KR, at] = dot_nt(eye, both).astype(BF)

    def landed(n):
        rows = TILE if n < CHUNKS - 1 else TILE - RPB
        part = recvb.at[pl.ds(n * TILE, rows), :]
        pltpu.make_async_copy(part, part, recv_sem.at[n]).wait()

    for n in range(HEAD):
        landed(n)
        moved = dot(placing[n], recvb[n * TILE:(n + 1) * TILE, :])
        if n == 0:
            total[...] = moved
        elif n < HEAD - 1:
            total[...] += moved
        else:
            field[...] = (total[...] + moved).astype(BF)
    partial = []
    for g in range(GROUPS):
        partial.append(own_lanes(lambda s: leafv[g * HALF + s], field[:, lanes_of(g)]))

    def level_part(j, g, half):
        x = comb[j, g, half * KR:(half + 1) * KR, :]
        part = slice(2 * half * KR, 2 * (half + 1) * KR)
        return own_lanes(lambda s: mixv[j, g * HALF + s, :, part], jnp.concatenate([x, x], axis=0))

    for n in range(HEAD, CHUNKS):
        landed(n)
    mine = recvb.at[pl.ds(RB - RPB, RPB), :]
    pltpu.make_async_copy(mine, mine, own_sem).wait()
    copies, coeffs = [[None] * GROUPS for _ in range(LEVELS)], []
    for g in range(GROUPS):
        rest = own_lanes(
            lambda s: turned[(g * HALF + s) * KR:(g * HALF + s + 1) * KR, :], recvb[HEAD * TILE:, lanes_of(g)]
        )
        copies[0][g] = exchange(0, g, partial[g] + rest)
    loads[6].wait()
    loads[7].wait()
    for j in range(LEVELS):
        partial = [level_part(j, g, 0) for g in range(GROUPS)]
        for g in range(GROUPS):
            copies[j][g].wait_recv()
            coeff = partial[g] + level_part(j, g, 1)
            if j + 1 < LEVELS:
                copies[j + 1][g] = exchange(j + 1, g, coeff)
            else:
                coeffs.append(coeff)
    for g in range(GROUPS):
        out[g] = jnp.transpose(coeffs[g]).astype(BF)
    for row in copies:
        for copy in row:
            copy.wait_send()
    left = recvb.at[pl.ds(0, RB - RPB), :]
    pltpu.make_async_copy(left, left, send_sem).wait()


def expand(coeff, top, out, block, sem):
    row_slot = iota((WIDE, KR), 0) & (HALF - 1)
    spread = []
    for g in range(GROUPS):
        rows = coeff[g].astype(F32)
        spread.append(jnp.concatenate(
            [jnp.where(row_slot == s, rows, 0.0).astype(BF) for s in range(HALF)], axis=1
        ))
    stores = []
    for n in range(LB // PART):
        at = pl.ds(n * PART, PART)
        for g in range(GROUPS):
            wanted = top[g * HALF * KR:(g + 1) * HALF * KR, at]
            block[:, g * HALF:(g + 1) * HALF, at] = dot(spread[g], wanted).reshape(COLS, HALF, PART)
        copy = pltpu.make_async_copy(block.at[:, :, at], out.at[:, :, at], sem.at[n])
        copy.start()
        stores.append(copy)
    for copy in stores:
        copy.wait()


def per_device(fourier, cycle_lat, order_table, leaf_op, level_op, skeleton, top_op):
    positions = jnp.asarray(np.repeat(np.array(PARTNERS, np.int32), RPB).reshape(1, RB))
    hbm = pl.BlockSpec(memory_space=pltpu.HBM)
    dma = pltpu.SemaphoreType.DMA
    coeff, top_turned = pl.pallas_call(
        analyse,
        out_shape=(
            jax.ShapeDtypeStruct((GROUPS, WIDE, KR), BF),
            jax.ShapeDtypeStruct((SLOTS * KR, LB), BF),
        ),
        in_specs=[hbm] * 8,
        out_specs=[pl.BlockSpec(memory_space=pltpu.VMEM)] * 2,
        scratch_shapes=[
            pltpu.VMEM((SLOTS, LB, KR), BF),
            pltpu.VMEM((COLS, ORDERS, ROWS), BF),
            pltpu.VMEM((2 * DEVICES, 128), I32),
            pltpu.VMEM((1, ORDERS), I32),
            pltpu.VMEM((SLOTS, KR, RB), BF),
            pltpu.VMEM((LEVELS, SLOTS, KR, 4 * KR), BF),
            pltpu.VMEM((LEVELS * SLOTS, KR), I32),
            pltpu.VMEM((1, RB), I32),
            pltpu.VMEM((OWNERS * GROUPS, WIDE, ROWS), F32),
            pltpu.VMEM((OWNERS, ROWS, GROUPS * WIDE), BF),
            pltpu.VMEM((RB, GROUPS * WIDE), BF),
            pltpu.VMEM((CHUNKS, RB, TILE), BF),
            pltpu.VMEM((SLOTS * KR, TAIL * TILE), BF),
            pltpu.VMEM((RB, GROUPS * WIDE), F32),
            pltpu.VMEM((RB, GROUPS * WIDE), BF),
            pltpu.VMEM((LEVELS, GROUPS, 2 * KR, WIDE), BF),
            dma((9,)),
            dma,
            dma((CHUNKS,)),
            dma,
            dma((LEVELS, GROUPS)),
            dma((LEVELS, GROUPS)),
        ],
        compiler_params=pltpu.CompilerParams(
            collective_id=0, has_side_effects=True, vmem_limit_bytes=44 * 1024 * 1024
        ),
    )(*(
        pltpu.with_memory_space_constraint(x, pltpu.HBM)
        for x in (
            fourier,
            cycle_lat.reshape(2 * DEVICES, 128),
            order_table.reshape(1, ORDERS),
            leaf_op,
            level_op[:, 0],
            skeleton.reshape(LEVELS * SLOTS, KR),
            positions,
            top_op,
        )
    ))
    return pl.pallas_call(
        expand,
        out_shape=jax.ShapeDtypeStruct((COLS, SLOTS, LB), F32),
        in_specs=[pl.BlockSpec(memory_space=pltpu.VMEM)] * 2,
        out_specs=pl.BlockSpec(memory_space=pl.ANY),
        scratch_shapes=[pltpu.VMEM((COLS, SLOTS, LB), F32), dma((LB // PART,))],
        compiler_params=pltpu.CompilerParams(vmem_limit_bytes=16 * 1024 * 1024),
    )(coeff, top_turned)


def solution(mesh):
    return jax.shard_map(
        per_device,
        mesh=mesh,
        in_specs=(
            P(None, None, ("blk", "order")),
            P(),
            P(),
            P("order", None, "blk"),
            P(None, "blk", "order", None, None),
            P(None, "blk", "order", None),
            P("order", "blk", None),
        ),
        out_specs=P(None, "order", "blk"),
        check_vma=False,
    )
```
